128 devices in a mesh: layer: 8 (over x, core), feat: 16 (over y, z).
Axes of the slice: x: 4, y: 4, z: 4, core: 2. Of those that a mesh axis runs over, the one named last changes fastest.
Arguments:
- acts_in: bfloat16 [8, 256, 3584], P('layer', 'feat'), may hold values from -6 to 6
- targets: bfloat16 [8, 256, 3584], P('layer', 'feat'), may hold values from -6 to 6
- enc_weight: bfloat16 [128, 3584, 1536], P(('layer', 'feat')), may hold values from -0.09375 to 0.09375
- dec_weight: bfloat16 [128, 1536, 3584], P(('layer', 'feat')), may hold values from -0.0390625 to 0.0390625
- thresholds: float32 [128, 1536], P(('layer', 'feat')), may hold values from 0 to 0.5
- skip_weight: bfloat16 [8, 3584, 3584], P('layer', 'feat'), may hold values from -0.09375 to 0.09375
- dec_bias: float32 [8, 3584], P('layer'), may hold values from -3 to 3
- owner: int32 [128], replicated, may hold values from 0 to 7, as said below
Outputs:
- errors: bfloat16 [8, 256, 3584], P('layer', 'feat')
The draws below stay inside these ranges and needn't reach their ends.
Inputs may be any that keep to these rules, and one draw needn't show every extreme that they name: `owner`: blocks are numbered group by group, 16 to a group; a block of group g belongs to layer g or a later one; at least half of each group's blocks belong to its own layer, and the last group's all do; some block of group 0 belongs to the last layer.
All inputs are finite; a program needn't handle non-finite values.
Results may differ from the reference program's by a relative error of at most 0.0059.
Values may be sent and summed in bfloat16 or wider, within the bound.
No kernel may reach another device: no remote copies, remote signals or barrier semaphores. Data moves between devices by JAX's collectives and lax.ppermute only.
A program may use at most 192 MiB of HBM per device.

```python
import jax
import jax.numpy as jnp
from jax import lax

D = 3584
FEAT_DEV = 1536
TOKENS = 256
LAYERS = 8
BLOCKS = 128
N_LAYER = 8
N_FEAT = 16


def draw_owner(key, part):
    key = jax.random.fold_in(key, 7)
    first, second = jax.random.split(key)
    scores = jax.random.randint(first, (N_LAYER, N_FEAT), 0, 1 << 20) * N_FEAT + jnp.arange(N_FEAT, dtype=jnp.int32)[None, :]
    ranks = jnp.argsort(jnp.argsort(scores, axis=1), axis=1)
    keep = ranks < N_FEAT // 2
    groups = jnp.arange(N_LAYER, dtype=jnp.int32)[:, None] * jnp.ones((1, N_FEAT), jnp.int32)
    spread = jax.random.randint(second, (N_LAYER, N_FEAT), 0, 1 << 20)
    lent = groups + spread % (N_LAYER - groups)
    wrapped = (groups == 0) & (ranks == N_FEAT // 2)
    lent = jnp.where(wrapped, N_LAYER - 1, lent)
    return jnp.where(keep, groups, lent).reshape(-1).astype(jnp.int32)


def block_levels(key, shape, cuts, low, largest):
    factor_of, own = 1.0, jax.random.fold_in(key, 6)
    for dim, parts in cuts:
        heights = jnp.exp(jax.random.uniform(jax.random.fold_in(own, dim), (parts,), jnp.float32, low / len(cuts), largest / len(cuts)))
        factor_of = factor_of * jnp.repeat(heights, shape[dim] // parts).reshape([-1 if axis == dim else 1 for axis in range(len(shape))])
    return factor_of


def noise(key, dims, width, bound, pieces=(), kind=jnp.bfloat16):
    drawn = jax.random.normal(key, dims, jnp.float32) * width
    if len(pieces) > 0:
        drawn = block_levels(key, dims, pieces, -0.22, 0.18) * drawn
    return jnp.clip(drawn, min=-bound, max=bound).astype(kind)


def setup_inputs(seed: int = 0) -> dict:
    splits = jax.random.split(jax.random.key(seed), 9)
    acts_in = noise(splits[0], (LAYERS, TOKENS, D), 1.0, 6.0, ((0, 8), (1, 16)))
    targets = noise(splits[1], (LAYERS, TOKENS, D), 1.0, 6.0, ((0, 8), (1, 16)))
    enc_weight = noise(splits[2], (BLOCKS, D, FEAT_DEV), D ** -0.5, 0.09375, ((0, 128),))
    dec_weight = noise(splits[3], (BLOCKS, FEAT_DEV, D), (16 * FEAT_DEV) ** -0.5, 0.0390625, ((0, 128),))
    thresholds = jnp.clip(0.5 * jax.random.uniform(splits[4], (BLOCKS, FEAT_DEV), jnp.float32) ** block_levels(splits[4], (BLOCKS, FEAT_DEV), ((0, 128),), -0.2, 0.2), 0.0, 0.5)
    skip_weight = noise(splits[5], (LAYERS, D, D), D ** -0.5, 0.09375, ((0, 8), (1, 16)))
    dec_bias = noise(splits[6], (LAYERS, D), 0.5, 3.0, ((0, 8),), jnp.float32)
    owner = draw_owner(jax.random.fold_in(splits[8], 71), 0)
    return {"acts_in": acts_in, "targets": targets, "enc_weight": enc_weight, "dec_weight": dec_weight, "thresholds": thresholds, "skip_weight": skip_weight, "dec_bias": dec_bias, "owner": owner}


def reference(acts_in, targets, enc_weight, dec_weight, thresholds, skip_weight, dec_bias, owner):
    def one_block(recon, index):
        layer_id = owner[index]
        rows = lax.dynamic_index_in_dim(acts_in, layer_id, 0, keepdims=False)
        pre = jnp.dot(rows, enc_weight[index], preferred_element_type=jnp.float32) - thresholds[index][None, :]
        act = jnp.maximum(pre, 0.0).astype(jnp.bfloat16)
        part = jnp.dot(act, dec_weight[index], preferred_element_type=jnp.float32)
        current = lax.dynamic_index_in_dim(recon, layer_id, 0, keepdims=False)
        recon = lax.dynamic_update_index_in_dim(recon, current + part, layer_id, 0)
        return recon, None

    start = jnp.zeros((LAYERS, TOKENS, D), jnp.float32)
    recon, unused = lax.scan(one_block, start, jnp.arange(BLOCKS, dtype=jnp.int32))

    def skip_layer(pair):
        return jnp.dot(pair[0], pair[1], preferred_element_type=jnp.float32)

    skipped = lax.map(skip_layer, (acts_in, skip_weight))
    total = recon + skipped + dec_bias[:, None, :]
    return (total - targets.astype(jnp.float32)).astype(jnp.bfloat16)
```

```python
import jax
import jax.numpy as jnp
from jax import lax
from jax.experimental import pallas as pl
from jax.experimental.pallas import tpu as pltpu
from jax.sharding import PartitionSpec as P

BF = jnp.bfloat16
F32 = jnp.float32


def pick_rows(source, index):
    count, (_, rows, width) = index.shape[0], source.shape

    def kernel(index_ref, source_ref, out_ref, sem):
        copies = [
            pltpu.make_async_copy(source_ref.at[index_ref[n]], out_ref.at[n], sem.at[n]) for n in range(count)
        ]
        for copy in copies:
            copy.start()
        for copy in copies:
            copy.wait()

    return pl.pallas_call(
        kernel,
        out_shape=jax.ShapeDtypeStruct((count, rows, width), source.dtype),
        in_specs=[pl.BlockSpec(memory_space=pltpu.SMEM), pl.BlockSpec(memory_space=pl.ANY)],
        out_specs=pl.BlockSpec(memory_space=pl.ANY),
        scratch_shapes=[pltpu.SemaphoreType.DMA((count,))],
        cost_estimate=pl.CostEstimate(flops=0, bytes_accessed=2 * count * rows * width * 2, transcendentals=0),
    )(index, source)


def sum_by_owner(parts, index, slots):
    count, rows, width = parts.shape
    step = width // 4

    def kernel(index_ref, parts_ref, out_ref, total):
        total[...] = jnp.zeros_like(total)
        for n in range(count):
            slot = index_ref[n]
            total[slot] = total[slot] + parts_ref[n].astype(F32)
        out_ref[...] = total[...].astype(out_ref.dtype)

    return pl.pallas_call(
        kernel,
        grid=(width // step,),
        out_shape=jax.ShapeDtypeStruct((slots, rows, width), BF),
        in_specs=[
            pl.BlockSpec(memory_space=pltpu.SMEM),
            pl.BlockSpec((count, rows, step), lambda i: (0, 0, i)),
        ],
        out_specs=pl.BlockSpec((slots, rows, step), lambda i: (0, 0, i)),
        scratch_shapes=[pltpu.VMEM((slots, rows, step), F32)],
        cost_estimate=pl.CostEstimate(flops=count * rows * width, bytes_accessed=(count + slots) * rows * width * 2, transcendentals=0),
    )(index, parts)


def per_device(acts_in, targets, enc_weight, dec_weight, thresholds, skip_weight, dec_bias, owner):
    width = lax.axis_size("feat")
    layers = lax.axis_size("layer")
    group = lax.axis_index("layer")
    shard, depth = acts_in.shape[1:]
    tokens = shard * width
    span = skip_weight.shape[1]
    mine = lax.dynamic_slice_in_dim(owner, group * width, width)

    cut = acts_in[0].reshape(shard, width, span).transpose(1, 0, 2)
    columns = lax.all_to_all(cut, "feat", 0, 0).reshape(tokens, span)
    skipped = jnp.dot(columns, skip_weight[0], preferred_element_type=F32)
    skip_sum = lax.psum_scatter(skipped, "feat", scatter_dimension=0, tiled=True)

    shards = lax.all_gather(acts_in[0], "layer", axis=0)
    sent = pick_rows(shards, mine)
    rows = lax.all_to_all(sent, "feat", 0, 0).reshape(tokens, depth)

    pre = jnp.dot(rows, enc_weight[0], preferred_element_type=F32) - thresholds[0][None, :]
    act = jnp.maximum(pre, 0.0).astype(BF)
    part = jnp.dot(act, dec_weight[0], preferred_element_type=F32).astype(BF)

    back = lax.all_to_all(part.reshape(width, shard, depth), "feat", 0, 0)
    slots = sum_by_owner(back, mine, layers)
    home = lax.all_to_all(slots, "layer", 0, 0)
    recon = jnp.sum(home.astype(F32), axis=0) + skip_sum
    total = recon + dec_bias[0][None, :] - targets[0].astype(F32)
    return total.astype(BF)[None]


def solution(mesh):
    placed = (
        P("layer", "feat", None),
        P("layer", "feat", None),
        P(("layer", "feat"), None, None),
        P(("layer", "feat"), None, None),
        P(("layer", "feat"), None),
        P("layer", "feat", None),
        P("layer", None),
        P(),
    )
    return jax.shard_map(
        per_device, mesh=mesh, in_specs=placed, out_specs=P("layer", "feat", None), check_vma=False
    )
```

```python
import functools

import jax
import jax.numpy as jnp
from jax import lax
from jax.experimental import pallas as pl
from jax.experimental.pallas import tpu as pltpu
from jax.sharding import PartitionSpec as P

BF = jnp.bfloat16
F32 = jnp.float32
MIB = 1 << 20
VMEM_LIMIT = 40 * MIB
WEIGHTS_LIMIT = 56 * MIB


def whole(memory_space):
    return pl.BlockSpec(memory_space=memory_space)


def pick_rows(near, far, place, cut):
    count, span = cut.shape[0], cut.shape[2]
    slots, rows, depth = near.shape
    padded = depth + -(-span // 128) * 128

    def kernel(place_ref, near_ref, far_ref, cut_ref, out_ref):
        for n in range(count):
            slot = place_ref[n]

            @pl.when(slot < slots)
            def _():
                out_ref[n, :, :depth] = near_ref[slot]

            @pl.when(slot >= slots)
            def _():
                out_ref[n, :, :depth] = far_ref[slot - slots]

            out_ref[n, :, depth : depth + span] = cut_ref[n]
            if padded > depth + span:
                out_ref[n, :, depth + span :] = jnp.zeros((rows, padded - depth - span), out_ref.dtype)

    return pl.pallas_call(
        kernel,
        out_shape=jax.ShapeDtypeStruct((count, rows, padded), near.dtype),
        in_specs=[whole(pltpu.SMEM)] + [whole(pltpu.VMEM)] * 3,
        out_specs=whole(pltpu.VMEM),
        compiler_params=pltpu.CompilerParams(vmem_limit_bytes=VMEM_LIMIT),
        cost_estimate=pl.CostEstimate(flops=0, bytes_accessed=2 * count * rows * padded * 2, transcendentals=0),
    )(place, near, far, cut)


def sum_by_place(parts, place, slots, after):
    count, rows, width = parts.shape
    step = 512

    def kernel(place_ref, parts_ref, after_ref, near_ref, far_ref, total):
        total[...] = jnp.zeros_like(total)
        for n in range(count):
            slot = place_ref[n]
            total[slot] = total[slot] + parts_ref[n].astype(F32)
        near_ref[...] = total[:slots].astype(BF)
        far_ref[...] = total[slots:].astype(BF)

    block = pl.BlockSpec((slots, rows, step), lambda i: (0, 0, i))
    return pl.pallas_call(
        kernel,
        grid=(width // step,),
        out_shape=[jax.ShapeDtypeStruct((slots, rows, width), BF)] * 2,
        in_specs=[whole(pltpu.SMEM), pl.BlockSpec((count, rows, step), lambda i: (0, 0, i)), whole(pl.ANY)],
        out_specs=[block, block],
        scratch_shapes=[pltpu.VMEM((2 * slots, rows, step), F32)],
        compiler_params=pltpu.CompilerParams(vmem_limit_bytes=VMEM_LIMIT),
        cost_estimate=pl.CostEstimate(flops=count * rows * width, bytes_accessed=(count + 2 * slots) * rows * width * 2, transcendentals=0),
    )(place, parts, after)


def encode_decode(x, enc, thresholds, dec, width, after):
    tokens, depth = x.shape[0], enc.shape[1]
    features = enc.shape[2]
    enc_cut, dec_cut = 512, 896
    enc_turns, dec_turns = features // enc_cut, width // dec_cut

    def kernel(x_ref, enc_ref, thr_ref, dec_ref, after_ref, act_ref, part_ref, enc_buf, dec_buf, enc_sem, dec_sem):
        def fetch_enc(n):
            at = pl.ds(n * enc_cut, enc_cut)
            return pltpu.make_async_copy(enc_ref.at[0, :, at], enc_buf.at[n], enc_sem.at[n])

        def fetch_dec(n):
            at = pl.ds(n * dec_cut, dec_cut)
            return pltpu.make_async_copy(dec_ref.at[0, :, at], dec_buf.at[n], dec_sem.at[n])

        for n in range(enc_turns):
            fetch_enc(n).start()
        for n in range(dec_turns):
            fetch_dec(n).start()
        for n in range(enc_turns):
            fetch_enc(n).wait()
            at = slice(n * enc_cut, (n + 1) * enc_cut)
            pre = jnp.dot(x_ref[:, :depth], enc_buf[n], preferred_element_type=F32) - thr_ref[:, at]
            act_ref[:, at] = jnp.maximum(pre, 0.0).astype(BF)
        for n in range(dec_turns):
            fetch_dec(n).wait()
            at = slice(n * dec_cut, (n + 1) * dec_cut)
            part_ref[:, at] = jnp.dot(act_ref[...], dec_buf[n], preferred_element_type=F32).astype(BF)

    return pl.pallas_call(
        kernel,
        out_shape=[jax.ShapeDtypeStruct((tokens, features), BF), jax.ShapeDtypeStruct((tokens, width), BF)],
        in_specs=[whole(pltpu.VMEM), whole(pl.ANY), whole(pltpu.VMEM), whole(pl.ANY), whole(pl.ANY)],
        out_specs=[whole(pltpu.VMEM)] * 2,
        scratch_shapes=[
            pltpu.VMEM((enc_turns, depth, enc_cut), BF),
            pltpu.VMEM((dec_turns, features, dec_cut), BF),
            pltpu.SemaphoreType.DMA((enc_turns,)),
            pltpu.SemaphoreType.DMA((dec_turns,)),
        ],
        compiler_params=pltpu.CompilerParams(vmem_limit_bytes=WEIGHTS_LIMIT),
        cost_estimate=pl.CostEstimate(flops=2 * tokens * features * (depth + width), bytes_accessed=features * (depth + width) * 2, transcendentals=0),
    )(x, enc, thresholds, dec, after)


def decode_rest(act, dec, begin, after):
    tokens, features = act.shape
    width = dec.shape[2] - begin
    cut = width // 2
    turns = width // cut

    def kernel(act_ref, dec_ref, after_ref, part_ref, dec_buf, dec_sem):
        def fetch(n):
            at = pl.ds(begin + n * cut, cut)
            return pltpu.make_async_copy(dec_ref.at[0, :, at], dec_buf.at[n], dec_sem.at[n])

        for n in range(turns):
            fetch(n).start()
        for n in range(turns):
            fetch(n).wait()
            at = slice(n * cut, (n + 1) * cut)
            part_ref[:, at] = jnp.dot(act_ref[...], dec_buf[n], preferred_element_type=F32).astype(BF)

    return pl.pallas_call(
        kernel,
        out_shape=jax.ShapeDtypeStruct((tokens, width), BF),
        in_specs=[whole(pltpu.VMEM), whole(pl.ANY), whole(pl.ANY)],
        out_specs=whole(pltpu.VMEM),
        scratch_shapes=[pltpu.VMEM((turns, features, cut), BF), pltpu.SemaphoreType.DMA((turns,))],
        compiler_params=pltpu.CompilerParams(vmem_limit_bytes=WEIGHTS_LIMIT),
        cost_estimate=pl.CostEstimate(flops=2 * tokens * features * width, bytes_accessed=features * width * 2, transcendentals=0),
    )(act, dec, after)


PIECES = 1


def per_device(chips, across, down, acts_in, targets, enc_weight, dec_weight, thresholds, skip_weight, dec_bias, owner):
    layers, width = 2 * chips, across * down
    group = lax.axis_index("layer")
    chip, core = group // 2, group % 2
    shard, depth = acts_in.shape[1:]
    tokens = shard * width
    span = skip_weight.shape[1]
    mine = lax.dynamic_slice_in_dim(owner, group * width, width)
    place = mine // 2 - chip + chips * (mine % 2 != core).astype(jnp.int32)
    swap = [(i, i ^ 1) for i in range(layers)]

    cut = acts_in[0].reshape(shard, width, span).transpose(1, 0, 2)

    later = [
        lax.ppermute(acts_in[0], "layer", [(i, i - 2 * s) for i in range(2 * s, layers)]) for s in range(1, chips)
    ]
    near = jnp.stack([acts_in[0], *later])
    far = lax.ppermute(near, "layer", swap)
    sent = pick_rows(near, far, place, cut)
    rows = lax.all_to_all(sent, "feat", 0, 0).reshape(tokens, sent.shape[2])
    skipped = jnp.dot(rows[:, depth : depth + span], skip_weight[0], preferred_element_type=F32).astype(BF)
    by_across = [[y * down + z for y in range(across)] for z in range(down)]
    by_down = [[y * down + z for z in range(down)] for y in range(across)]
    halfway = lax.psum_scatter(skipped, "feat", scatter_dimension=0, axis_index_groups=by_across, tiled=True)

    act, part = encode_decode(rows, enc_weight, thresholds, dec_weight, depth // PIECES, skipped)
    skip_sum = lax.psum_scatter(halfway.astype(F32), "feat", scatter_dimension=0, axis_index_groups=by_down, tiled=True)
    parts = [part]
    if PIECES == 2:
        parts.append(decode_rest(act, dec_weight, depth // PIECES, halfway))

    backs = [lax.all_to_all(part.reshape(width, shard, depth // PIECES), "feat", 0, 0) for part in parts]
    outs = []
    for back in backs:
        kept, given = sum_by_place(back, place, chips, outs[-1] if outs else halfway)
        taken = lax.ppermute(given, "layer", swap)
        pair = (kept.astype(F32) + taken.astype(F32)).astype(BF)
        arrived = [
            lax.ppermute(pair[s], "layer", [(i, i + 2 * s) for i in range(layers - 2 * s)]) for s in range(1, chips)
        ]
        outs.append(sum((a.astype(F32) for a in arrived), pair[0].astype(F32)))
    recon = jnp.concatenate(outs, axis=1) + skip_sum
    total = recon + dec_bias[0][None, :] - targets[0].astype(F32)
    return total.astype(BF)[None]


def solution(mesh):
    placed = (
        P("layer", "feat", None),
        P("layer", "feat", None),
        P(("layer", "feat"), None, None),
        P(("layer", "feat"), None, None),
        P(("layer", "feat"), None),
        P("layer", "feat", None),
        P("layer", None),
        P(),
    )
    chips, across = mesh.shape["layer"] // 2, 4
    down = mesh.shape["feat"] // across
    return jax.shard_map(
        functools.partial(per_device, chips, across, down),
        mesh=mesh,
        in_specs=placed,
        out_specs=P("layer", "feat", None),
        check_vma=False,
    )
```

```python
import functools

import jax
import jax.numpy as jnp
from jax import lax
from jax.experimental import pallas as pl
from jax.experimental.pallas import tpu as pltpu
from jax.sharding import PartitionSpec as P

BF = jnp.bfloat16
F32 = jnp.float32
MIB = 1 << 20
VMEM_LIMIT = 40 * MIB
WEIGHTS_LIMIT = 56 * MIB


def whole(memory_space):
    return pl.BlockSpec(memory_space=memory_space)


def pick_rows(near, far, place, cut):
    count, span = cut.shape[0], cut.shape[2]
    slots, rows, depth = near.shape
    padded = depth + -(-span // 128) * 128

    def kernel(place_ref, near_ref, far_ref, cut_ref, out_ref):
        for n in range(count):
            slot = place_ref[n]

            @pl.when(slot < slots)
            def _():
                out_ref[n, :, :depth] = near_ref[slot]

            @pl.when(slot >= slots)
            def _():
                out_ref[n, :, :depth] = far_ref[slot - slots]

            out_ref[n, :, depth : depth + span] = cut_ref[n]
            if padded > depth + span:
                out_ref[n, :, depth + span :] = jnp.zeros((rows, padded - depth - span), out_ref.dtype)

    return pl.pallas_call(
        kernel,
        out_shape=jax.ShapeDtypeStruct((count, rows, padded), near.dtype),
        in_specs=[whole(pltpu.SMEM)] + [whole(pltpu.VMEM)] * 3,
        out_specs=whole(pltpu.VMEM),
        compiler_params=pltpu.CompilerParams(vmem_limit_bytes=VMEM_LIMIT),
        cost_estimate=pl.CostEstimate(flops=0, bytes_accessed=2 * count * rows * padded * 2, transcendentals=0),
    )(place, near, far, cut)


def sum_by_place(parts, place, slots, after):
    count, rows, width = parts.shape
    step = 512

    def kernel(place_ref, parts_ref, after_ref, near_ref, far_ref, total):
        total[...] = jnp.zeros_like(total)
        for n in range(count):
            slot = place_ref[n]
            total[slot] = total[slot] + parts_ref[n].astype(F32)
        near_ref[...] = total[:slots].astype(BF)
        far_ref[...] = total[slots:].astype(BF)

    block = pl.BlockSpec((slots, rows, step), lambda i: (0, 0, i))
    return pl.pallas_call(
        kernel,
        grid=(width // step,),
        out_shape=[jax.ShapeDtypeStruct((slots, rows, width), BF)] * 2,
        in_specs=[whole(pltpu.SMEM), pl.BlockSpec((count, rows, step), lambda i: (0, 0, i)), whole(pl.ANY)],
        out_specs=[block, block],
        scratch_shapes=[pltpu.VMEM((2 * slots, rows, step), F32)],
        compiler_params=pltpu.CompilerParams(vmem_limit_bytes=VMEM_LIMIT),
        cost_estimate=pl.CostEstimate(flops=count * rows * width, bytes_accessed=(count + 2 * slots) * rows * width * 2, transcendentals=0),
    )(place, parts, after)


def encode_decode(x, enc, thresholds, dec, width, after):
    tokens, depth = x.shape[0], enc.shape[1]
    features = enc.shape[2]
    enc_cut, dec_cut = 512, 896
    enc_turns, dec_turns = features // enc_cut, width // dec_cut

    def kernel(x_ref, enc_ref, thr_ref, dec_ref, after_ref, act_ref, part_ref, enc_buf, dec_buf, enc_sem, dec_sem):
        def fetch_enc(n):
            at = pl.ds(n * enc_cut, enc_cut)
            return pltpu.make_async_copy(enc_ref.at[0, :, at], enc_buf.at[n], enc_sem.at[n])

        def fetch_dec(n):
            at = pl.ds(n * dec_cut, dec_cut)
            return pltpu.make_async_copy(dec_ref.at[0, :, at], dec_buf.at[n], dec_sem.at[n])

        for n in range(enc_turns):
            fetch_enc(n).start()
        for n in range(dec_turns):
            fetch_dec(n).start()
        for n in range(enc_turns):
            fetch_enc(n).wait()
            at = slice(n * enc_cut, (n + 1) * enc_cut)
            pre = jnp.dot(x_ref[:, :depth], enc_buf[n], preferred_element_type=F32) - thr_ref[:, at]
            act_ref[:, at] = jnp.maximum(pre, 0.0).astype(BF)
        for n in range(dec_turns):
            fetch_dec(n).wait()
            at = slice(n * dec_cut, (n + 1) * dec_cut)
            part_ref[:, at] = jnp.dot(act_ref[...], dec_buf[n], preferred_element_type=F32).astype(BF)

    return pl.pallas_call(
        kernel,
        out_shape=[jax.ShapeDtypeStruct((tokens, features), BF), jax.ShapeDtypeStruct((tokens, width), BF)],
        in_specs=[whole(pltpu.VMEM), whole(pl.ANY), whole(pltpu.VMEM), whole(pl.ANY), whole(pl.ANY)],
        out_specs=[whole(pltpu.VMEM)] * 2,
        scratch_shapes=[
            pltpu.VMEM((enc_turns, depth, enc_cut), BF),
            pltpu.VMEM((dec_turns, features, dec_cut), BF),
            pltpu.SemaphoreType.DMA((enc_turns,)),
            pltpu.SemaphoreType.DMA((dec_turns,)),
        ],
        compiler_params=pltpu.CompilerParams(vmem_limit_bytes=WEIGHTS_LIMIT),
        cost_estimate=pl.CostEstimate(flops=2 * tokens * features * (depth + width), bytes_accessed=features * (depth + width) * 2, transcendentals=0),
    )(x, enc, thresholds, dec, after)


def decode_rest(act, dec, begin, after):
    tokens, features = act.shape
    width = dec.shape[2] - begin
    cut = width // 2
    turns = width // cut

    def kernel(act_ref, dec_ref, after_ref, part_ref, dec_buf, dec_sem):
        def fetch(n):
            at = pl.ds(begin + n * cut, cut)
            return pltpu.make_async_copy(dec_ref.at[0, :, at], dec_buf.at[n], dec_sem.at[n])

        for n in range(turns):
            fetch(n).start()
        for n in range(turns):
            fetch(n).wait()
            at = slice(n * cut, (n + 1) * cut)
            part_ref[:, at] = jnp.dot(act_ref[...], dec_buf[n], preferred_element_type=F32).astype(BF)

    return pl.pallas_call(
        kernel,
        out_shape=jax.ShapeDtypeStruct((tokens, width), BF),
        in_specs=[whole(pltpu.VMEM), whole(pl.ANY), whole(pl.ANY)],
        out_specs=whole(pltpu.VMEM),
        scratch_shapes=[pltpu.VMEM((turns, features, cut), BF), pltpu.SemaphoreType.DMA((turns,))],
        compiler_params=pltpu.CompilerParams(vmem_limit_bytes=WEIGHTS_LIMIT),
        cost_estimate=pl.CostEstimate(flops=2 * tokens * features * width, bytes_accessed=features * width * 2, transcendentals=0),
    )(act, dec, after)


def skip_product(rows, weight, start, begin, width, after):
    tokens, span = rows.shape[0], weight.shape[1]

    def kernel(rows_ref, weight_ref, after_ref, out_ref):
        out_ref[...] = jnp.dot(
            rows_ref[:, start : start + span], weight_ref[0, :, begin : begin + width], preferred_element_type=F32
        ).astype(BF)

    return pl.pallas_call(
        kernel,
        out_shape=jax.ShapeDtypeStruct((tokens, width), BF),
        in_specs=[whole(pltpu.VMEM), whole(pltpu.VMEM), whole(pl.ANY)],
        out_specs=whole(pltpu.VMEM),
        compiler_params=pltpu.CompilerParams(vmem_limit_bytes=VMEM_LIMIT),
        cost_estimate=pl.CostEstimate(flops=2 * tokens * span * width, bytes_accessed=(tokens + span) * width * 2, transcendentals=0),
    )(rows, weight, after)


PIECES = 1


def per_device(chips, across, down, acts_in, targets, enc_weight, dec_weight, thresholds, skip_weight, dec_bias, owner):
    layers, width = 2 * chips, across * down
    group = lax.axis_index("layer")
    chip, core = group // 2, group % 2
    shard, depth = acts_in.shape[1:]
    tokens = shard * width
    span = skip_weight.shape[1]
    mine = lax.dynamic_slice_in_dim(owner, group * width, width)
    place = mine // 2 - chip + chips * (mine % 2 != core).astype(jnp.int32)
    swap = [(i, i ^ 1) for i in range(layers)]

    cut = acts_in[0].reshape(shard, width, span).transpose(1, 0, 2)

    later = [
        lax.ppermute(acts_in[0], "layer", [(i, i - 2 * s) for i in range(2 * s, layers)]) for s in range(1, chips)
    ]
    near = jnp.stack([acts_in[0], *later])
    far = lax.ppermute(near, "layer", swap)
    sent = pick_rows(near, far, place, cut)
    rows = lax.all_to_all(sent, "feat", 0, 0).reshape(tokens, sent.shape[2])
    half = depth // 2
    skip_a = skip_product(rows, skip_weight, depth, 0, half, place)
    skip_a_back = lax.all_to_all(skip_a.reshape(width, shard, half), "feat", 0, 0)

    _, part = encode_decode(rows, enc_weight, thresholds, dec_weight, depth, skip_a)
    part, skip_a_back = lax.optimization_barrier((part, skip_a_back))

    back = lax.all_to_all(part.reshape(width, shard, depth), "feat", 0, 0)
    skip_b = skip_product(rows, skip_weight, depth, half, half, back)
    skip_b_back = lax.all_to_all(skip_b.reshape(width, shard, half), "feat", 0, 0)
    kept, given = sum_by_place(back, place, chips, skip_b)
    taken = lax.ppermute(given, "layer", swap)
    pair = (kept.astype(F32) + taken.astype(F32)).astype(BF)
    arrived = [
        lax.ppermute(pair[s], "layer", [(i, i + 2 * s) for i in range(layers - 2 * s)]) for s in range(1, chips)
    ]
    recon = sum((a.astype(F32) for a in arrived), pair[0].astype(F32))
    skip_sum = jnp.concatenate(
        [jnp.sum(skip_a_back.astype(F32), axis=0), jnp.sum(skip_b_back.astype(F32), axis=0)], axis=1
    )
    recon = recon + skip_sum
    total = recon + dec_bias[0][None, :] - targets[0].astype(F32)
    return total.astype(BF)[None]


def solution(mesh):
    placed = (
        P("layer", "feat", None),
        P("layer", "feat", None),
        P(("layer", "feat"), None, None),
        P(("layer", "feat"), None, None),
        P(("layer", "feat"), None),
        P("layer", "feat", None),
        P("layer", None),
        P(),
    )
    chips, across = mesh.shape["layer"] // 2, 4
    down = mesh.shape["feat"] // across
    return jax.shard_map(
        functools.partial(per_device, chips, across, down),
        mesh=mesh,
        in_specs=placed,
        out_specs=P("layer", "feat", None),
        check_vma=False,
    )
```

```python
import functools

import jax
import jax.numpy as jnp
from jax import lax
from jax.experimental import pallas as pl
from jax.experimental.pallas import tpu as pltpu
from jax.sharding import PartitionSpec as P

BF = jnp.bfloat16
F32 = jnp.float32
MIB = 1 << 20
VMEM_LIMIT = 40 * MIB
WEIGHTS_LIMIT = 56 * MIB


def whole(memory_space):
    return pl.BlockSpec(memory_space=memory_space)


def pick_rows(near, far, place, cut):
    count, span = cut.shape[0], cut.shape[2]
    slots, rows, depth = near.shape
    padded = depth + -(-span // 128) * 128

    def kernel(place_ref, near_ref, far_ref, cut_ref, out_ref):
        for n in range(count):
            slot = place_ref[n]

            @pl.when(slot < slots)
            def _():
                out_ref[n, :, :depth] = near_ref[slot]

            @pl.when(slot >= slots)
            def _():
                out_ref[n, :, :depth] = far_ref[slot - slots]

            out_ref[n, :, depth : depth + span] = cut_ref[n]
            if padded > depth + span:
                out_ref[n, :, depth + span :] = jnp.zeros((rows, padded - depth - span), out_ref.dtype)

    return pl.pallas_call(
        kernel,
        out_shape=jax.ShapeDtypeStruct((count, rows, padded), near.dtype),
        in_specs=[whole(pltpu.SMEM)] + [whole(pltpu.VMEM)] * 3,
        out_specs=whole(pltpu.VMEM),
        compiler_params=pltpu.CompilerParams(vmem_limit_bytes=VMEM_LIMIT),
        cost_estimate=pl.CostEstimate(flops=0, bytes_accessed=2 * count * rows * padded * 2, transcendentals=0),
    )(place, near, far, cut)


def sum_by_place(parts, place, slots, after):
    count, rows, width = parts.shape
    step = 512

    def kernel(place_ref, parts_ref, after_ref, near_ref, far_ref, total):
        total[...] = jnp.zeros_like(total)
        for n in range(count):
            slot = place_ref[n]
            total[slot] = total[slot] + parts_ref[n].astype(F32)
        near_ref[...] = total[:slots].astype(BF)
        far_ref[...] = total[slots:].astype(BF)

    block = pl.BlockSpec((slots, rows, step), lambda i: (0, 0, i))
    return pl.pallas_call(
        kernel,
        grid=(width // step,),
        out_shape=[jax.ShapeDtypeStruct((slots, rows, width), BF)] * 2,
        in_specs=[whole(pltpu.SMEM), pl.BlockSpec((count, rows, step), lambda i: (0, 0, i)), whole(pl.ANY)],
        out_specs=[block, block],
        scratch_shapes=[pltpu.VMEM((2 * slots, rows, step), F32)],
        compiler_params=pltpu.CompilerParams(vmem_limit_bytes=VMEM_LIMIT),
        cost_estimate=pl.CostEstimate(flops=count * rows * width, bytes_accessed=(count + 2 * slots) * rows * width * 2, transcendentals=0),
    )(place, parts, after)


def encode_decode(x, enc, thresholds, dec, width, after):
    tokens, depth = x.shape[0], enc.shape[1]
    features = enc.shape[2]
    enc_cut, dec_cut = 512, 896
    enc_turns, dec_turns = features // enc_cut, width // dec_cut

    def kernel(x_ref, enc_ref, thr_ref, dec_ref, after_ref, act_ref, part_ref, enc_buf, dec_buf, enc_sem, dec_sem):
        def fetch_enc(n):
            at = pl.ds(n * enc_cut, enc_cut)
            return pltpu.make_async_copy(enc_ref.at[0, :, at], enc_buf.at[n], enc_sem.at[n])

        def fetch_dec(n):
            at = pl.ds(n * dec_cut, dec_cut)
            return pltpu.make_async_copy(dec_ref.at[0, :, at], dec_buf.at[n], dec_sem.at[n])

        for n in range(enc_turns):
            fetch_enc(n).start()
        for n in range(dec_turns):
            fetch_dec(n).start()
        for n in range(enc_turns):
            fetch_enc(n).wait()
            at = slice(n * enc_cut, (n + 1) * enc_cut)
            pre = jnp.dot(x_ref[:, :depth], enc_buf[n], preferred_element_type=F32) - thr_ref[:, at]
            act_ref[:, at] = jnp.maximum(pre, 0.0).astype(BF)
        for n in range(dec_turns):
            fetch_dec(n).wait()
            at = slice(n * dec_cut, (n + 1) * dec_cut)
            part_ref[:, at] = jnp.dot(act_ref[...], dec_buf[n], preferred_element_type=F32).astype(BF)

    return pl.pallas_call(
        kernel,
        out_shape=[jax.ShapeDtypeStruct((tokens, features), BF), jax.ShapeDtypeStruct((tokens, width), BF)],
        in_specs=[whole(pltpu.VMEM), whole(pl.ANY), whole(pltpu.VMEM), whole(pl.ANY), whole(pl.ANY)],
        out_specs=[whole(pltpu.VMEM)] * 2,
        scratch_shapes=[
            pltpu.VMEM((enc_turns, depth, enc_cut), BF),
            pltpu.VMEM((dec_turns, features, dec_cut), BF),
            pltpu.SemaphoreType.DMA((enc_turns,)),
            pltpu.SemaphoreType.DMA((dec_turns,)),
        ],
        compiler_params=pltpu.CompilerParams(vmem_limit_bytes=WEIGHTS_LIMIT),
        cost_estimate=pl.CostEstimate(flops=2 * tokens * features * (depth + width), bytes_accessed=features * (depth + width) * 2, transcendentals=0),
    )(x, enc, thresholds, dec, after)


def decode_rest(act, dec, begin, after):
    tokens, features = act.shape
    width = dec.shape[2] - begin
    cut = width // 2
    turns = width // cut

    def kernel(act_ref, dec_ref, after_ref, part_ref, dec_buf, dec_sem):
        def fetch(n):
            at = pl.ds(begin + n * cut, cut)
            return pltpu.make_async_copy(dec_ref.at[0, :, at], dec_buf.at[n], dec_sem.at[n])

        for n in range(turns):
            fetch(n).start()
        for n in range(turns):
            fetch(n).wait()
            at = slice(n * cut, (n + 1) * cut)
            part_ref[:, at] = jnp.dot(act_ref[...], dec_buf[n], preferred_element_type=F32).astype(BF)

    return pl.pallas_call(
        kernel,
        out_shape=jax.ShapeDtypeStruct((tokens, width), BF),
        in_specs=[whole(pltpu.VMEM), whole(pl.ANY), whole(pl.ANY)],
        out_specs=whole(pltpu.VMEM),
        scratch_shapes=[pltpu.VMEM((turns, features, cut), BF), pltpu.SemaphoreType.DMA((turns,))],
        compiler_params=pltpu.CompilerParams(vmem_limit_bytes=WEIGHTS_LIMIT),
        cost_estimate=pl.CostEstimate(flops=2 * tokens * features * width, bytes_accessed=features * width * 2, transcendentals=0),
    )(act, dec, after)


def skip_product(rows, weight, start, split):
    tokens, span, width = rows.shape[0], weight.shape[1], weight.shape[2]

    def kernel(rows_ref, weight_ref, first_ref, second_ref):
        x = rows_ref[:, start : start + span]
        first_ref[...] = jnp.dot(x, weight_ref[0, :, :split], preferred_element_type=F32).astype(BF)
        second_ref[...] = jnp.dot(x, weight_ref[0, :, split:], preferred_element_type=F32).astype(BF)

    return pl.pallas_call(
        kernel,
        out_shape=[jax.ShapeDtypeStruct((tokens, w), BF) for w in (split, width - split)],
        in_specs=[whole(pltpu.VMEM)] * 2,
        out_specs=[whole(pltpu.VMEM)] * 2,
        compiler_params=pltpu.CompilerParams(vmem_limit_bytes=VMEM_LIMIT),
        cost_estimate=pl.CostEstimate(flops=2 * tokens * span * width, bytes_accessed=(tokens + span) * width * 2, transcendentals=0),
    )(rows, weight)


SPLIT = 2304


def per_device(chips, across, down, acts_in, targets, enc_weight, dec_weight, thresholds, skip_weight, dec_bias, owner):
    layers, width = 2 * chips, across * down
    group = lax.axis_index("layer")
    chip, core = group // 2, group % 2
    shard, depth = acts_in.shape[1:]
    tokens = shard * width
    span = skip_weight.shape[1]
    mine = lax.dynamic_slice_in_dim(owner, group * width, width)
    place = mine // 2 - chip + chips * (mine % 2 != core).astype(jnp.int32)
    swap = [(i, i ^ 1) for i in range(layers)]

    cut = acts_in[0].reshape(shard, width, span).transpose(1, 0, 2)

    later = [
        lax.ppermute(acts_in[0], "layer", [(i, i - 2 * s) for i in range(2 * s, layers)]) for s in range(1, chips)
    ]
    near = jnp.stack([acts_in[0], *later])
    far = lax.ppermute(near, "layer", swap)
    sent = pick_rows(near, far, place, cut)
    rows = lax.all_to_all(sent, "feat", 0, 0).reshape(tokens, sent.shape[2])
    half = SPLIT
    skip_a, skip_b = skip_product(rows, skip_weight, depth, half)
    skip_a_back = lax.all_to_all(skip_a.reshape(width, shard, half), "feat", 0, 0)

    _, part = encode_decode(rows, enc_weight, thresholds, dec_weight, depth, skip_a)
    part, skip_a_back = lax.optimization_barrier((part, skip_a_back))

    back = lax.all_to_all(part.reshape(width, shard, depth), "feat", 0, 0)
    back, skip_b = lax.optimization_barrier((back, skip_b))
    skip_b_back = lax.all_to_all(skip_b.reshape(width, shard, depth - half), "feat", 0, 0)
    kept, given = sum_by_place(back, place, chips, skip_b)
    taken = lax.ppermute(given, "layer", swap)
    pair = (kept.astype(F32) + taken.astype(F32)).astype(BF)
    arrived = [
        lax.ppermute(pair[s], "layer", [(i, i + 2 * s) for i in range(layers - 2 * s)]) for s in range(1, chips)
    ]
    recon = sum((a.astype(F32) for a in arrived), pair[0].astype(F32))
    skip_sum = jnp.concatenate(
        [jnp.sum(skip_a_back.astype(F32), axis=0), jnp.sum(skip_b_back.astype(F32), axis=0)], axis=1
    )
    recon = recon + skip_sum
    total = recon + dec_bias[0][None, :] - targets[0].astype(F32)
    return total.astype(BF)[None]


def solution(mesh):
    placed = (
        P("layer", "feat", None),
        P("layer", "feat", None),
        P(("layer", "feat"), None, None),
        P(("layer", "feat"), None, None),
        P(("layer", "feat"), None),
        P("layer", "feat", None),
        P("layer", None),
        P(),
    )
    chips, across = mesh.shape["layer"] // 2, 4
    down = mesh.shape["feat"] // across
    return jax.shard_map(
        functools.partial(per_device, chips, across, down),
        mesh=mesh,
        in_specs=placed,
        out_specs=P("layer", "feat", None),
        check_vma=False,
    )
```

```python
import functools

import jax
import jax.numpy as jnp
from jax import lax
from jax.experimental import pallas as pl
from jax.experimental.pallas import tpu as pltpu
from jax.sharding import PartitionSpec as P

BF = jnp.bfloat16
F32 = jnp.float32
MIB = 1 << 20
VMEM_LIMIT = 40 * MIB
WEIGHTS_LIMIT = 56 * MIB


def whole(memory_space):
    return pl.BlockSpec(memory_space=memory_space)


def pick_rows(near, far, place, cut):
    count, span = cut.shape[0], cut.shape[2]
    slots, rows, depth = near.shape
    padded = depth + -(-span // 128) * 128

    def kernel(place_ref, near_ref, far_ref, cut_ref, out_ref):
        for n in range(count):
            slot = place_ref[n]

            @pl.when(slot < slots)
            def _():
                out_ref[n, :, :depth] = near_ref[slot]

            @pl.when(slot >= slots)
            def _():
                out_ref[n, :, :depth] = far_ref[slot - slots]

            out_ref[n, :, depth : depth + span] = cut_ref[n]
            if padded > depth + span:
                out_ref[n, :, depth + span :] = jnp.zeros((rows, padded - depth - span), out_ref.dtype)

    return pl.pallas_call(
        kernel,
        out_shape=jax.ShapeDtypeStruct((count, rows, padded), near.dtype),
        in_specs=[whole(pltpu.SMEM)] + [whole(pltpu.VMEM)] * 3,
        out_specs=whole(pltpu.VMEM),
        compiler_params=pltpu.CompilerParams(vmem_limit_bytes=VMEM_LIMIT),
        cost_estimate=pl.CostEstimate(flops=0, bytes_accessed=2 * count * rows * padded * 2, transcendentals=0),
    )(place, near, far, cut)


def sum_by_place(parts, place, slots, after):
    count, rows, width = parts.shape
    step = 512

    def kernel(place_ref, parts_ref, after_ref, near_ref, far_ref, total):
        total[...] = jnp.zeros_like(total)
        for n in range(count):
            slot = place_ref[n]
            total[slot] = total[slot] + parts_ref[n].astype(F32)
        near_ref[...] = total[:slots].astype(BF)
        far_ref[...] = total[slots:].astype(BF)

    block = pl.BlockSpec((slots, rows, step), lambda i: (0, 0, i))
    return pl.pallas_call(
        kernel,
        grid=(width // step,),
        out_shape=[jax.ShapeDtypeStruct((slots, rows, width), BF)] * 2,
        in_specs=[whole(pltpu.SMEM), pl.BlockSpec((count, rows, step), lambda i: (0, 0, i)), whole(pl.ANY)],
        out_specs=[block, block],
        scratch_shapes=[pltpu.VMEM((2 * slots, rows, step), F32)],
        compiler_params=pltpu.CompilerParams(vmem_limit_bytes=VMEM_LIMIT),
        cost_estimate=pl.CostEstimate(flops=count * rows * width, bytes_accessed=(count + 2 * slots) * rows * width * 2, transcendentals=0),
    )(place, parts, after)


def encode_decode(x, enc, thresholds, dec, width, after):
    tokens, depth = x.shape[0], enc.shape[1]
    features = enc.shape[2]
    enc_cut, dec_cut = 512, 896
    enc_turns, dec_turns = features // enc_cut, width // dec_cut

    def kernel(x_ref, enc_ref, thr_ref, dec_ref, after_ref, act_ref, part_ref, enc_buf, dec_buf, enc_sem, dec_sem):
        def fetch_enc(n):
            at = pl.ds(n * enc_cut, enc_cut)
            return pltpu.make_async_copy(enc_ref.at[0, :, at], enc_buf.at[n], enc_sem.at[n])

        def fetch_dec(n):
            at = pl.ds(n * dec_cut, dec_cut)
            return pltpu.make_async_copy(dec_ref.at[0, :, at], dec_buf.at[n], dec_sem.at[n])

        for n in range(enc_turns):
            fetch_enc(n).start()
        for n in range(dec_turns):
            fetch_dec(n).start()
        for n in range(enc_turns):
            fetch_enc(n).wait()
            at = slice(n * enc_cut, (n + 1) * enc_cut)
            pre = jnp.dot(x_ref[:, :depth], enc_buf[n], preferred_element_type=F32) - thr_ref[:, at]
            act_ref[:, at] = jnp.maximum(pre, 0.0).astype(BF)
        for n in range(dec_turns):
            fetch_dec(n).wait()
            at = slice(n * dec_cut, (n + 1) * dec_cut)
            part_ref[:, at] = jnp.dot(act_ref[...], dec_buf[n], preferred_element_type=F32).astype(BF)

    return pl.pallas_call(
        kernel,
        out_shape=[jax.ShapeDtypeStruct((tokens, features), BF), jax.ShapeDtypeStruct((tokens, width), BF)],
        in_specs=[whole(pltpu.VMEM), whole(pl.ANY), whole(pltpu.VMEM), whole(pl.ANY), whole(pl.ANY)],
        out_specs=[whole(pltpu.VMEM)] * 2,
        scratch_shapes=[
            pltpu.VMEM((enc_turns, depth, enc_cut), BF),
            pltpu.VMEM((dec_turns, features, dec_cut), BF),
            pltpu.SemaphoreType.DMA((enc_turns,)),
            pltpu.SemaphoreType.DMA((dec_turns,)),
        ],
        compiler_params=pltpu.CompilerParams(vmem_limit_bytes=WEIGHTS_LIMIT),
        cost_estimate=pl.CostEstimate(flops=2 * tokens * features * (depth + width), bytes_accessed=features * (depth + width) * 2, transcendentals=0),
    )(x, enc, thresholds, dec, after)


def decode_rest(act, dec, begin, after):
    tokens, features = act.shape
    width = dec.shape[2] - begin
    cut = width // 2
    turns = width // cut

    def kernel(act_ref, dec_ref, after_ref, part_ref, dec_buf, dec_sem):
        def fetch(n):
            at = pl.ds(begin + n * cut, cut)
            return pltpu.make_async_copy(dec_ref.at[0, :, at], dec_buf.at[n], dec_sem.at[n])

        for n in range(turns):
            fetch(n).start()
        for n in range(turns):
            fetch(n).wait()
            at = slice(n * cut, (n + 1) * cut)
            part_ref[:, at] = jnp.dot(act_ref[...], dec_buf[n], preferred_element_type=F32).astype(BF)

    return pl.pallas_call(
        kernel,
        out_shape=jax.ShapeDtypeStruct((tokens, width), BF),
        in_specs=[whole(pltpu.VMEM), whole(pl.ANY), whole(pl.ANY)],
        out_specs=whole(pltpu.VMEM),
        scratch_shapes=[pltpu.VMEM((turns, features, cut), BF), pltpu.SemaphoreType.DMA((turns,))],
        compiler_params=pltpu.CompilerParams(vmem_limit_bytes=WEIGHTS_LIMIT),
        cost_estimate=pl.CostEstimate(flops=2 * tokens * features * width, bytes_accessed=features * width * 2, transcendentals=0),
    )(act, dec, after)


def skip_product(rows, weight, start, split):
    tokens, span, width = rows.shape[0], weight.shape[1], weight.shape[2]

    def kernel(rows_ref, weight_ref, first_ref, second_ref):
        x = rows_ref[:, start : start + span]
        first_ref[...] = jnp.dot(x, weight_ref[0, :, :split], preferred_element_type=F32).astype(BF)
        second_ref[...] = jnp.dot(x, weight_ref[0, :, split:], preferred_element_type=F32).astype(BF)

    return pl.pallas_call(
        kernel,
        out_shape=[jax.ShapeDtypeStruct((tokens, w), BF) for w in (split, width - split)],
        in_specs=[whole(pltpu.VMEM)] * 2,
        out_specs=[whole(pltpu.VMEM)] * 2,
        compiler_params=pltpu.CompilerParams(vmem_limit_bytes=VMEM_LIMIT),
        cost_estimate=pl.CostEstimate(flops=2 * tokens * span * width, bytes_accessed=(tokens + span) * width * 2, transcendentals=0),
    )(rows, weight)


SPLIT = 2304


def per_device(chips, across, down, acts_in, targets, enc_weight, dec_weight, thresholds, skip_weight, dec_bias, owner):
    layers, width = 2 * chips, across * down
    group = lax.axis_index("layer")
    chip, core = group // 2, group % 2
    shard, depth = acts_in.shape[1:]
    tokens = shard * width
    span = skip_weight.shape[1]
    mine = lax.dynamic_slice_in_dim(owner, group * width, width)
    place = mine // 2 - chip + chips * (mine % 2 != core).astype(jnp.int32)
    swap = [(i, i ^ 1) for i in range(layers)]

    cut = acts_in[0].reshape(shard, width, span).transpose(1, 0, 2)

    same_core = [[2 * x + c for x in range(chips)] for c in range(2)]
    near = lax.all_gather(acts_in[0], "layer", axis=0, axis_index_groups=same_core)
    far = lax.ppermute(near, "layer", swap)
    sent = pick_rows(near, far, mine // 2 + chips * (mine % 2 != core).astype(jnp.int32), cut)
    rows = lax.all_to_all(sent, "feat", 0, 0).reshape(tokens, sent.shape[2])
    half = SPLIT
    skip_a, skip_b = skip_product(rows, skip_weight, depth, half)
    skip_a_back = lax.all_to_all(skip_a.reshape(width, shard, half), "feat", 0, 0)

    _, part = encode_decode(rows, enc_weight, thresholds, dec_weight, depth, skip_a)
    part, skip_a_back = lax.optimization_barrier((part, skip_a_back))

    back = lax.all_to_all(part.reshape(width, shard, depth), "feat", 0, 0)
    back, skip_b = lax.optimization_barrier((back, skip_b))
    skip_b_back = lax.all_to_all(skip_b.reshape(width, shard, depth - half), "feat", 0, 0)
    kept, given = sum_by_place(back, place, chips, skip_b)
    taken = lax.ppermute(given, "layer", swap)
    pair = (kept.astype(F32) + taken.astype(F32)).astype(BF)
    arrived = [
        lax.ppermute(pair[s], "layer", [(i, i + 2 * s) for i in range(layers - 2 * s)]) for s in range(1, chips)
    ]
    recon = sum((a.astype(F32) for a in arrived), pair[0].astype(F32))
    skip_sum = jnp.concatenate(
        [jnp.sum(skip_a_back.astype(F32), axis=0), jnp.sum(skip_b_back.astype(F32), axis=0)], axis=1
    )
    recon = recon + skip_sum
    total = recon + dec_bias[0][None, :] - targets[0].astype(F32)
    return total.astype(BF)[None]


def solution(mesh):
    placed = (
        P("layer", "feat", None),
        P("layer", "feat", None),
        P(("layer", "feat"), None, None),
        P(("layer", "feat"), None, None),
        P(("layer", "feat"), None),
        P("layer", "feat", None),
        P("layer", None),
        P(),
    )
    chips, across = mesh.shape["layer"] // 2, 4
    down = mesh.shape["feat"] // across
    return jax.shard_map(
        functools.partial(per_device, chips, across, down),
        mesh=mesh,
        in_specs=placed,
        out_specs=P("layer", "feat", None),
        check_vma=False,
    )
```

```python
import functools

import jax
import jax.numpy as jnp
from jax import lax
from jax.experimental import pallas as pl
from jax.experimental.pallas import tpu as pltpu
from jax.sharding import PartitionSpec as P

BF = jnp.bfloat16
F32 = jnp.float32
MIB = 1 << 20
VMEM_LIMIT = 40 * MIB
WEIGHTS_LIMIT = 56 * MIB


def whole(memory_space):
    return pl.BlockSpec(memory_space=memory_space)


def pick_rows(near, far, place, cut):
    count, span = cut.shape[0], cut.shape[2]
    slots, rows, depth = near.shape
    padded = depth + -(-span // 128) * 128

    def kernel(place_ref, near_ref, far_ref, cut_ref, out_ref):
        for n in range(count):
            slot = place_ref[n]

            @pl.when(slot < slots)
            def _():
                out_ref[n, :, :depth] = near_ref[slot]

            @pl.when(slot >= slots)
            def _():
                out_ref[n, :, :depth] = far_ref[slot - slots]

            out_ref[n, :, depth : depth + span] = cut_ref[n]
            if padded > depth + span:
                out_ref[n, :, depth + span :] = jnp.zeros((rows, padded - depth - span), out_ref.dtype)

    return pl.pallas_call(
        kernel,
        out_shape=jax.ShapeDtypeStruct((count, rows, padded), near.dtype),
        in_specs=[whole(pltpu.SMEM)] + [whole(pltpu.VMEM)] * 3,
        out_specs=whole(pltpu.VMEM),
        compiler_params=pltpu.CompilerParams(vmem_limit_bytes=VMEM_LIMIT),
        cost_estimate=pl.CostEstimate(flops=0, bytes_accessed=2 * count * rows * padded * 2, transcendentals=0),
    )(place, near, far, cut)


def sum_by_place(parts, place, slots, after):
    count, rows, width = parts.shape
    step = 512

    def kernel(place_ref, parts_ref, after_ref, near_ref, far_ref, total):
        total[...] = jnp.zeros_like(total)
        for n in range(count):
            slot = place_ref[n]
            total[slot] = total[slot] + parts_ref[n].astype(F32)
        near_ref[...] = total[:slots].astype(BF)
        far_ref[...] = total[slots:].astype(BF)

    block = pl.BlockSpec((slots, rows, step), lambda i: (0, 0, i))
    return pl.pallas_call(
        kernel,
        grid=(width // step,),
        out_shape=[jax.ShapeDtypeStruct((slots, rows, width), BF)] * 2,
        in_specs=[whole(pltpu.SMEM), pl.BlockSpec((count, rows, step), lambda i: (0, 0, i)), whole(pl.ANY)],
        out_specs=[block, block],
        scratch_shapes=[pltpu.VMEM((2 * slots, rows, step), F32)],
        compiler_params=pltpu.CompilerParams(vmem_limit_bytes=VMEM_LIMIT),
        cost_estimate=pl.CostEstimate(flops=count * rows * width, bytes_accessed=(count + 2 * slots) * rows * width * 2, transcendentals=0),
    )(place, parts, after)


def encode_decode(x, enc, thresholds, dec, width, after):
    tokens, depth = x.shape[0], enc.shape[1]
    features = enc.shape[2]
    enc_cut, dec_cut = 512, 896
    enc_turns, dec_turns = features // enc_cut, width // dec_cut

    def kernel(x_ref, enc_ref, thr_ref, dec_ref, after_ref, act_ref, part_ref, enc_buf, dec_buf, enc_sem, dec_sem):
        def fetch_enc(n):
            at = pl.ds(n * enc_cut, enc_cut)
            return pltpu.make_async_copy(enc_ref.at[0, :, at], enc_buf.at[n], enc_sem.at[n])

        def fetch_dec(n):
            at = pl.ds(n * dec_cut, dec_cut)
            return pltpu.make_async_copy(dec_ref.at[0, :, at], dec_buf.at[n], dec_sem.at[n])

        for n in range(enc_turns):
            fetch_enc(n).start()
        for n in range(dec_turns):
            fetch_dec(n).start()
        for n in range(enc_turns):
            fetch_enc(n).wait()
            at = slice(n * enc_cut, (n + 1) * enc_cut)
            pre = jnp.dot(x_ref[:, :depth], enc_buf[n], preferred_element_type=F32) - thr_ref[:, at]
            act_ref[:, at] = jnp.maximum(pre, 0.0).astype(BF)
        for n in range(dec_turns):
            fetch_dec(n).wait()
            at = slice(n * dec_cut, (n + 1) * dec_cut)
            part_ref[:, at] = jnp.dot(act_ref[...], dec_buf[n], preferred_element_type=F32).astype(BF)

    return pl.pallas_call(
        kernel,
        out_shape=[jax.ShapeDtypeStruct((tokens, features), BF), jax.ShapeDtypeStruct((tokens, width), BF)],
        in_specs=[whole(pltpu.VMEM), whole(pl.ANY), whole(pltpu.VMEM), whole(pl.ANY), whole(pl.ANY)],
        out_specs=[whole(pltpu.VMEM)] * 2,
        scratch_shapes=[
            pltpu.VMEM((enc_turns, depth, enc_cut), BF),
            pltpu.VMEM((dec_turns, features, dec_cut), BF),
            pltpu.SemaphoreType.DMA((enc_turns,)),
            pltpu.SemaphoreType.DMA((dec_turns,)),
        ],
        compiler_params=pltpu.CompilerParams(vmem_limit_bytes=WEIGHTS_LIMIT),
        cost_estimate=pl.CostEstimate(flops=2 * tokens * features * (depth + width), bytes_accessed=features * (depth + width) * 2, transcendentals=0),
    )(x, enc, thresholds, dec, after)


def decode_rest(act, dec, begin, after):
    tokens, features = act.shape
    width = dec.shape[2] - begin
    cut = width // 2
    turns = width // cut

    def kernel(act_ref, dec_ref, after_ref, part_ref, dec_buf, dec_sem):
        def fetch(n):
            at = pl.ds(begin + n * cut, cut)
            return pltpu.make_async_copy(dec_ref.at[0, :, at], dec_buf.at[n], dec_sem.at[n])

        for n in range(turns):
            fetch(n).start()
        for n in range(turns):
            fetch(n).wait()
            at = slice(n * cut, (n + 1) * cut)
            part_ref[:, at] = jnp.dot(act_ref[...], dec_buf[n], preferred_element_type=F32).astype(BF)

    return pl.pallas_call(
        kernel,
        out_shape=jax.ShapeDtypeStruct((tokens, width), BF),
        in_specs=[whole(pltpu.VMEM), whole(pl.ANY), whole(pl.ANY)],
        out_specs=whole(pltpu.VMEM),
        scratch_shapes=[pltpu.VMEM((turns, features, cut), BF), pltpu.SemaphoreType.DMA((turns,))],
        compiler_params=pltpu.CompilerParams(vmem_limit_bytes=WEIGHTS_LIMIT),
        cost_estimate=pl.CostEstimate(flops=2 * tokens * features * width, bytes_accessed=features * width * 2, transcendentals=0),
    )(act, dec, after)


def skip_product(rows, weight, start, split):
    tokens, span, width = rows.shape[0], weight.shape[1], weight.shape[2]

    def kernel(rows_ref, weight_ref, first_ref, second_ref):
        x = rows_ref[:, start : start + span]
        first_ref[...] = jnp.dot(x, weight_ref[0, :, :split], preferred_element_type=F32).astype(BF)
        second_ref[...] = jnp.dot(x, weight_ref[0, :, split:], preferred_element_type=F32).astype(BF)

    return pl.pallas_call(
        kernel,
        out_shape=[jax.ShapeDtypeStruct((tokens, w), BF) for w in (split, width - split)],
        in_specs=[whole(pltpu.VMEM)] * 2,
        out_specs=[whole(pltpu.VMEM)] * 2,
        compiler_params=pltpu.CompilerParams(vmem_limit_bytes=VMEM_LIMIT),
        cost_estimate=pl.CostEstimate(flops=2 * tokens * span * width, bytes_accessed=(tokens + span) * width * 2, transcendentals=0),
    )(rows, weight)


SPLIT = 2304


def per_device(chips, across, down, acts_in, targets, enc_weight, dec_weight, thresholds, skip_weight, dec_bias, owner):
    layers, width = 2 * chips, across * down
    group = lax.axis_index("layer")
    chip, core = group // 2, group % 2
    shard, depth = acts_in.shape[1:]
    tokens = shard * width
    span = skip_weight.shape[1]
    mine = lax.dynamic_slice_in_dim(owner, group * width, width)
    place = mine // 2 - chip + chips * (mine % 2 != core).astype(jnp.int32)
    swap = [(i, i ^ 1) for i in range(layers)]

    cut = acts_in[0].reshape(shard, width, span).transpose(1, 0, 2)

    same_core = [[2 * x + c for x in range(chips)] for c in range(2)]
    near = lax.all_gather(acts_in[0], "layer", axis=0, axis_index_groups=same_core)
    far = lax.ppermute(near, "layer", swap)
    sent = pick_rows(near, far, mine // 2 + chips * (mine % 2 != core).astype(jnp.int32), cut)
    sent = lax.optimization_barrier(sent)
    rows = lax.all_to_all(sent, "feat", 0, 0).reshape(tokens, sent.shape[2])
    half = SPLIT
    skip_a, skip_b = skip_product(rows, skip_weight, depth, half)
    skip_a_back = lax.all_to_all(skip_a.reshape(width, shard, half), "feat", 0, 0)

    _, part = encode_decode(rows, enc_weight, thresholds, dec_weight, depth, skip_a)
    part, skip_a_back = lax.optimization_barrier((part, skip_a_back))

    back = lax.all_to_all(part.reshape(width, shard, depth), "feat", 0, 0)
    back, skip_b = lax.optimization_barrier((back, skip_b))
    skip_b_back = lax.all_to_all(skip_b.reshape(width, shard, depth - half), "feat", 0, 0)
    kept, given = sum_by_place(back, place, chips, skip_b)
    taken = lax.ppermute(given, "layer", swap)
    pair = (kept.astype(F32) + taken.astype(F32)).astype(BF)
    arrived = [
        lax.ppermute(pair[s], "layer", [(i, i + 2 * s) for i in range(layers - 2 * s)]) for s in range(1, chips)
    ]
    recon = sum((a.astype(F32) for a in arrived), pair[0].astype(F32))
    skip_sum = jnp.concatenate(
        [jnp.sum(skip_a_back.astype(F32), axis=0), jnp.sum(skip_b_back.astype(F32), axis=0)], axis=1
    )
    recon = recon + skip_sum
    total = recon + dec_bias[0][None, :] - targets[0].astype(F32)
    return total.astype(BF)[None]


def solution(mesh):
    placed = (
        P("layer", "feat", None),
        P("layer", "feat", None),
        P(("layer", "feat"), None, None),
        P(("layer", "feat"), None, None),
        P(("layer", "feat"), None),
        P("layer", "feat", None),
        P("layer", None),
        P(),
    )
    chips, across = mesh.shape["layer"] // 2, 4
    down = mesh.shape["feat"] // across
    return jax.shard_map(
        functools.partial(per_device, chips, across, down),
        mesh=mesh,
        in_specs=placed,
        out_specs=P("layer", "feat", None),
        check_vma=False,
    )
```
